256 devices in a mesh: tm: 32 (over y, x, core), space: 8 (over z).
Axes of the slice: x: 4, y: 4, z: 8, core: 2. Of those that a mesh axis runs over, the one named last changes fastest.
Arguments:
- queries: bfloat16 [131072, 1536], P(('tm', 'space')), may hold values from -6 to 6
- key_rows: bfloat16 [131072, 1536], P(('tm', 'space')), may hold values from -6 to 6
- value_rows: bfloat16 [131072, 1536], P(('tm', 'space')), may hold values from -6 to 6
- block_list: int32 [1024, 8], P(('tm', 'space')), may hold values from 0 to 1023, as said below
- block_count: int32 [1024], P(('tm', 'space')), may hold values from 1 to 8
Outputs:
- attended: bfloat16 [131072, 1536], P(('tm', 'space'))
The draws below stay inside these ranges and needn't reach their ends.
Inputs may be any that keep to these rules, and one draw needn't show every extreme that they name: `block_list`: the candidates of query tile t, which lies in frame f = t // 32 at block p = t % 32 of the frame and in slab s = p // 4, are: the blocks of frame f with in-frame index from s * 4 - 1 to (s + 1) * 4 that lie within the frame; and, for each b from 0 to 4 and each of the frames f - 2**b and f + 2**b that lie within the clip, its blocks with in-frame index s * 4 + j where j runs over 0 to 3 with j % 2 == b % 2. Every entry of row t, padded ones included, is such a candidate, the entries of a row are distinct, and the first entry is block t itself.
All inputs are finite; a program needn't handle non-finite values.
Results may differ from the reference program's by a relative error of at most 0.0044.
Values may be sent and summed in bfloat16 or wider, within the bound.
No kernel may reach another device: no remote copies, remote signals or barrier semaphores. Data moves between devices by JAX's collectives and lax.ppermute only.
A program may use at most 128 MiB of HBM per device.

```python
import jax
import jax.numpy as jnp
from jax import lax

HEADS = 12
HEAD = 128
D = 1536
BLOCK = 128
BLOCKS_DEV = 4
TM_BITS = 5
LIST = 8
FRAME_BLOCKS = 32
QTILES = 1024
TOKENS = 131072
N_TM = 32
N_SPACE = 8


def pair_fields(key):
    key_base = jax.random.fold_in(key, 11)
    key_one, key_two = jax.random.split(key_base, 2)
    query_field = jnp.clip(jax.random.normal(key_one, (TOKENS, D), jnp.float32), -6.0, 6.0)
    key_field = jnp.clip(jax.random.normal(key_two, (TOKENS, D), jnp.float32), -6.0, 6.0)
    return (query_field, key_field)


def draw_queries(key, part):
    return pair_fields(key)[0].astype(jnp.bfloat16)


def draw_key_rows(key, part):
    return pair_fields(key)[1].astype(jnp.bfloat16)


def mask_lists(key):
    key_base = jax.random.fold_in(key, 7)
    key_one, key_two = jax.random.split(key_base, 2)
    tile_ids = jnp.arange(QTILES, dtype=jnp.int32)
    frame_ids = tile_ids // FRAME_BLOCKS
    inner_ids = tile_ids % FRAME_BLOCKS
    slab_ids = inner_ids // BLOCKS_DEV
    local_ids = inner_ids % BLOCKS_DEV
    first_block = frame_ids * FRAME_BLOCKS + slab_ids * BLOCKS_DEV
    offsets = jnp.arange(BLOCKS_DEV + 2, dtype=jnp.int32) - 1
    near_ids = first_block[:, None] + offsets[None, :]
    near_ok = ((slab_ids[:, None] > 0) | (offsets[None, :] >= 0)) & ((slab_ids[:, None] < N_SPACE - 1) | (offsets[None, :] < BLOCKS_DEV))
    own_mark = offsets[None, :] == local_ids[:, None]
    id_parts = [near_ids]
    ok_parts = [near_ok]
    own_parts = [own_mark]
    picks_base = 2 * jnp.arange(BLOCKS_DEV // 2, dtype=jnp.int32)
    for bit_index in range(TM_BITS):
        for direction in (-1, 1):
            partner_frame = frame_ids + direction * (1 << bit_index)
            frame_ok = (partner_frame >= 0) & (partner_frame < N_TM)
            safe_frame = jnp.clip(partner_frame, 0, N_TM - 1)
            band_ids = safe_frame[:, None] * FRAME_BLOCKS + slab_ids[:, None] * BLOCKS_DEV + picks_base[None, :] + bit_index % 2
            id_parts.append(band_ids)
            ok_parts.append(jnp.broadcast_to(frame_ok[:, None], band_ids.shape))
            own_parts.append(jnp.zeros(band_ids.shape, dtype=bool))
    cand_ids = jnp.concatenate(id_parts, axis=1)
    cand_ok = jnp.concatenate(ok_parts, axis=1)
    cand_own = jnp.concatenate(own_parts, axis=1)
    width_cand = cand_ids.shape[1]
    ranks = jax.random.randint(key_one, (QTILES, width_cand), 0, 1 << 20) * width_cand + jnp.arange(width_cand, dtype=jnp.int32)[None, :]
    ranks = jnp.where(cand_own, -1, jnp.where(cand_ok, ranks, 1 << 30))
    picked = jnp.argsort(ranks, axis=1, stable=True)[:, :LIST]
    lists = jnp.take_along_axis(cand_ids, picked, axis=1).astype(jnp.int32)
    counts = jax.random.randint(key_two, (QTILES,), 1, LIST + 1)
    counts = jnp.where(tile_ids % 5 == 1, 1, counts)
    counts = jnp.where(tile_ids % 3 == 0, LIST, counts).astype(jnp.int32)
    return (lists, counts)


def draw_block_list(key, part):
    return mask_lists(key)[0]


def draw_block_count(key, part):
    return mask_lists(key)[1]


def shard_levels(rng, shape, cuts, low, largest):
    factor_of, own = 1.0, jax.random.fold_in(rng, 6)
    for dim, blocks in cuts:
        heights = jnp.exp(jax.random.uniform(jax.random.fold_in(own, dim), (blocks,), jnp.float32, low / len(cuts), largest / len(cuts)))
        factor_of = factor_of * jnp.repeat(heights, shape[dim] // blocks).reshape([-1 if axis == dim else 1 for axis in range(len(shape))])
    return factor_of


def scatter_about(rng, shape, width, bound, cuts=(), kind=jnp.bfloat16):
    loudness = shard_levels(rng, shape, cuts, -0.22, 0.18) if cuts else 1.0
    values = jax.random.normal(rng, shape, jnp.float32) * width * loudness
    return jnp.minimum(jnp.maximum(values, -bound), bound).astype(kind)


def setup_inputs(seed: int = 0) -> dict:
    key_of = jax.random.split(jax.random.key(seed), 6)
    queries = draw_queries(jax.random.fold_in(key_of[5], 71), 0)
    key_rows = draw_key_rows(jax.random.fold_in(key_of[5], 71), 0)
    value_rows = scatter_about(key_of[2], (TOKENS, D), 1.0, 6.0, ((0, 256),))
    block_list = draw_block_list(jax.random.fold_in(key_of[5], 71), 0)
    block_count = draw_block_count(jax.random.fold_in(key_of[5], 71), 0)
    return dict(queries=queries, key_rows=key_rows, value_rows=value_rows, block_list=block_list, block_count=block_count)


def reference(queries, key_rows, value_rows, block_list, block_count):
    inv_root = 1.0 / (HEAD ** 0.5)
    query_tiles = queries.reshape(QTILES, BLOCK, HEADS, HEAD)
    key_blocks = key_rows.reshape(QTILES, BLOCK, HEADS, HEAD)
    value_blocks = value_rows.reshape(QTILES, BLOCK, HEADS, HEAD)

    def tile_attend(packed):
        query_tile, picked, live_count = packed
        key_sel = key_blocks[picked].reshape(LIST * BLOCK, HEADS, HEAD)
        value_sel = value_blocks[picked].reshape(LIST * BLOCK, HEADS, HEAD)
        scores = jnp.einsum("qhd,khd->hqk", query_tile.astype(jnp.float32), key_sel.astype(jnp.float32)) * inv_root
        live_keys = (jnp.arange(LIST * BLOCK, dtype=jnp.int32) // BLOCK) < live_count
        scores = jnp.where(live_keys[None, None, :], scores, -1e30)
        row_max = jnp.max(scores, axis=-1, keepdims=True)
        weights = jnp.where(live_keys[None, None, :], jnp.exp(scores - row_max), 0.0)
        row_sum = jnp.sum(weights, axis=-1)
        rounded = lax.optimization_barrier(weights.astype(jnp.bfloat16))
        mixed_out = jnp.einsum("hqk,khd->qhd", rounded.astype(jnp.float32), value_sel.astype(jnp.float32))
        return (mixed_out / jnp.transpose(row_sum)[:, :, None]).astype(jnp.bfloat16)

    result = lax.map(tile_attend, (query_tiles, block_list, block_count))
    return result.reshape(TOKENS, D)
```

```python
import jax
import jax.numpy as jnp
from jax import lax
from jax.experimental import pallas as pl
from jax.experimental.pallas import tpu as pltpu
from jax.sharding import PartitionSpec as P

HEAD = 128
BLOCK = 128
ROWS = 4
COLS = 4
SPACE = 8
STEP_HEADS = 4
NEG = -1e30
AXES = ("tm", "space")
barrier = lax.optimization_barrier


def device(y, x, core, z):
    return ((y % ROWS * COLS + x % COLS) * 2 + core) * SPACE + z


def permute(cells, move):
    pairs = []
    for y in range(ROWS):
        for x in range(COLS):
            for core in range(2):
                for z in range(SPACE):
                    place = move(y, x, core, z)
                    if place is not None:
                        pairs.append((device(y, x, core, z), device(*place)))
    return lax.ppermute(cells, AXES, pairs)


def up(y, x, core, z):
    return (y + 1, x, core, z) if y < ROWS - 1 else None


def down(y, x, core, z):
    return (y - 1, x, core, z) if y > 0 else None


def right(y, x, core, z):
    return (y, x + 1, core, z) if x < COLS - 1 else None


def left(y, x, core, z):
    return (y, x - 1, core, z) if x > 0 else None


def around(y, x, core, z):
    if x == COLS - 1 and y > 0:
        return (y, 0, core, z)
    if x == 0 and y < ROWS - 1:
        return (y, COLS - 1, core, z)
    return None


def ring_first(y, x, core, z):
    return (y, x + 1, 0, z) if core == 1 else (y, x - 1, 1, z)


def ring_second(y, x, core, z):
    return (y, x + 1, 1, z) if core == 0 else (y, x - 1, 0, z)


def carry(y, x, core, z):
    if x == 0 and core == 0 and y < ROWS - 1:
        return (y + 1, x, core, z)
    if x == COLS - 1 and core == 1 and y > 0:
        return (y - 1, x, core, z)
    return None


def other_row(y, x, core, z):
    if x < COLS // 2:
        return (y + 1, x, core, z) if y < ROWS - 1 else None
    return (y - 1, x, core, z) if y > 0 else None


def half_way(y, x, core, z):
    return (y - 1, x, core, z) if x < COLS // 2 else (y + 1, x, core, z)


def other_core(y, x, core, z):
    return (y, x, 1 - core, z)


def next_slab(y, x, core, z):
    return (y, x, core, z + 1) if z < SPACE - 1 else None


def last_slab(y, x, core, z):
    return (y, x, core, z - 1) if z > 0 else None


def absorb(live_ref, tile, pair, key_of, value_of, q_ref, max_ref, sum_ref, acc_ref, first):
    scale = 1.4426950408889634 / HEAD**0.5
    low = jnp.where(live_ref[tile, 2 * pair] > 0, 0.0, NEG)
    high = jnp.where(live_ref[tile, 2 * pair + 1] > 0, 0.0, NEG)
    for head in range(STEP_HEADS):
        cols = slice(head * HEAD, (head + 1) * HEAD)
        query = q_ref[tile * BLOCK : (tile + 1) * BLOCK, cols]
        scores = lax.dot_general(
            key_of(cols), query, (((1,), (1,)), ((), ())), preferred_element_type=jnp.float32
        )
        scores = jnp.concatenate(
            [scores[:BLOCK] * scale + low, scores[BLOCK:] * scale + high], axis=0
        )
        top = jnp.max(scores, axis=0, keepdims=True)
        if not first:
            old = max_ref[tile, 0, head : head + 1, :]
            top = jnp.maximum(top, old)
        weights = jnp.exp2(scores - top)
        total = jnp.sum(weights, axis=0, keepdims=True)
        mixed = lax.dot_general(
            value_of(cols),
            weights.astype(jnp.bfloat16),
            (((0,), (0,)), ((), ())),
            preferred_element_type=jnp.float32,
        )
        if not first:
            fade = jnp.exp2(old - top)
            total = total + sum_ref[tile, 0, head : head + 1, :] * fade
            mixed = mixed + acc_ref[tile, cols, :] * fade
        max_ref[tile, 0, head : head + 1, :] = top
        sum_ref[tile, 0, head : head + 1, :] = total
        acc_ref[tile, cols, :] = mixed


def absorb_pairs(live_ref, tile, base, groups, q_ref, max_ref, sum_ref, acc_ref):
    for index, group in enumerate(groups):
        pair = base + index

        @pl.when(live_ref[tile, 2 * pair] + live_ref[tile, 2 * pair + 1] > 0)
        def _():
            absorb(
                live_ref,
                tile,
                pair,
                lambda cols: group[0, :, :, cols].reshape(2 * BLOCK, HEAD),
                lambda cols: group[1, :, :, cols].reshape(2 * BLOCK, HEAD),
                q_ref,
                max_ref,
                sum_ref,
                acc_ref,
                False,
            )


def early_kernel(live_ref, q_ref, k_ref, v_ref, below_ref, above_ref, *rest):
    groups, (max_ref, sum_ref, acc_ref) = rest[:-3], rest[-3:]
    tiles = q_ref.shape[0] // BLOCK

    def own(pair):
        rows = slice(2 * pair * BLOCK, (2 * pair + 2) * BLOCK)
        return (lambda cols: k_ref[rows, cols]), (lambda cols: v_ref[rows, cols])

    def halo(which):
        return lambda cols: jnp.concatenate([below_ref[which, :, cols], above_ref[which, :, cols]], axis=0)

    state = (q_ref, max_ref, sum_ref, acc_ref)
    for tile in range(tiles):
        mine = tile // 2
        absorb(live_ref, tile, mine, *own(mine), *state, True)
        for pair in range(tiles // 2):
            if pair != mine:

                @pl.when(live_ref[tile, 2 * pair] + live_ref[tile, 2 * pair + 1] > 0)
                def _():
                    absorb(live_ref, tile, pair, *own(pair), *state, False)

        edge = tiles // 2

        @pl.when(live_ref[tile, 2 * edge] + live_ref[tile, 2 * edge + 1] > 0)
        def _():
            absorb(live_ref, tile, edge, halo(0), halo(1), *state, False)

        absorb_pairs(live_ref, tile, edge + 1, groups, *state)


def late_kernel(live_ref, q_ref, old_max_ref, old_sum_ref, old_acc_ref, *rest):
    groups, (out_ref, max_ref, sum_ref, acc_ref) = rest[:-4], rest[-4:]
    tiles = q_ref.shape[0] // BLOCK
    max_ref[...] = old_max_ref[...]
    sum_ref[...] = old_sum_ref[...]
    acc_ref[...] = old_acc_ref[...]
    for tile in range(tiles):
        absorb_pairs(live_ref, tile, 0, groups, q_ref, max_ref, sum_ref, acc_ref)
        for head in range(STEP_HEADS):
            cols = slice(head * HEAD, (head + 1) * HEAD)
            done = acc_ref[tile, cols, :] / sum_ref[tile, 0, head : head + 1, :]
            out_ref[tile * BLOCK : (tile + 1) * BLOCK, cols] = done.T.astype(jnp.bfloat16)


def state_shapes(tiles, width):
    steps = width // HEAD // STEP_HEADS
    small = jax.ShapeDtypeStruct((tiles, steps, STEP_HEADS, BLOCK), jnp.float32)
    return small, small, jax.ShapeDtypeStruct((tiles, width, BLOCK), jnp.float32)


def state_specs(tiles):
    small = pl.BlockSpec((tiles, 1, STEP_HEADS, BLOCK), lambda i: (0, i, 0, 0))
    return [small, small, pl.BlockSpec((tiles, STEP_HEADS * HEAD, BLOCK), lambda i: (0, i, 0))]


def attend_early(live, queries, key_rows, value_rows, below, above, groups):
    rows, width = queries.shape
    tiles = rows // BLOCK
    wide = STEP_HEADS * HEAD
    flat = pl.BlockSpec((rows, wide), lambda i: (0, i))
    edge = pl.BlockSpec((2, BLOCK, wide), lambda i: (0, 0, i))
    pair = pl.BlockSpec((2, 2, BLOCK, wide), lambda i: (0, 0, 0, i))
    return pl.pallas_call(
        early_kernel,
        grid=(width // wide,),
        in_specs=[pl.BlockSpec(memory_space=pltpu.SMEM), flat, flat, flat, edge, edge]
        + [pair] * len(groups),
        out_specs=state_specs(tiles),
        out_shape=state_shapes(tiles, width),
        compiler_params=pltpu.CompilerParams(vmem_limit_bytes=56 * 1024 * 1024),
        cost_estimate=pl.CostEstimate(
            flops=6_400_000_000, bytes_accessed=25_000_000, transcendentals=6_000_000
        ),
        name="early",
    )(live, queries, key_rows, value_rows, below, above, *groups)


def attend_late(live, queries, state, groups):
    rows, width = queries.shape
    tiles = rows // BLOCK
    wide = STEP_HEADS * HEAD
    flat = pl.BlockSpec((rows, wide), lambda i: (0, i))
    pair = pl.BlockSpec((2, 2, BLOCK, wide), lambda i: (0, 0, 0, i))
    return pl.pallas_call(
        late_kernel,
        grid=(width // wide,),
        in_specs=[pl.BlockSpec(memory_space=pltpu.SMEM), flat]
        + state_specs(tiles)
        + [pair] * len(groups),
        out_specs=flat,
        out_shape=jax.ShapeDtypeStruct((rows, width), jnp.bfloat16),
        scratch_shapes=[
            pltpu.VMEM((tiles, 1, STEP_HEADS, BLOCK), jnp.float32),
            pltpu.VMEM((tiles, 1, STEP_HEADS, BLOCK), jnp.float32),
            pltpu.VMEM((tiles, wide, BLOCK), jnp.float32),
        ],
        compiler_params=pltpu.CompilerParams(vmem_limit_bytes=56 * 1024 * 1024),
        cost_estimate=pl.CostEstimate(
            flops=1_600_000_000, bytes_accessed=15_000_000, transcendentals=3_000_000
        ),
        name="late",
    )(live, queries, *state, *groups)


def shards(queries, key_rows, value_rows, block_list, block_count):
    rows, width = queries.shape
    blocks = rows // BLOCK
    frame_blocks = blocks * SPACE
    frame, slab = lax.axis_index("tm"), lax.axis_index("space")
    y, x, core = frame // (2 * COLS), frame // 2 % COLS, frame % 2

    shaped = jnp.stack([key_rows, value_rows]).reshape(2, blocks, BLOCK, width)
    even, odd, first, last = barrier(
        (shaped[:, 0::2], shaped[:, 1::2], shaped[:, 0], shaped[:, blocks - 1])
    )

    def after(cells, done):
        return barrier((cells, done))[0]

    from_down = permute(odd, up)
    from_up = permute(odd, down)
    near_chip = permute(even, ring_first)
    twin = permute(even, other_core)
    below = permute(last, next_slab)
    above = permute(after(first, twin), last_slab)
    two_chips = permute(near_chip, ring_second)
    from_left = permute(after(odd, below), right)
    from_right = permute(after(odd, above), left)
    half = permute(barrier((even, from_down, from_up))[0], half_way)
    carried = permute(barrier((near_chip, from_down, from_up))[0], carry)
    two_other = permute(two_chips, other_row)
    wrapped = permute(after(jnp.where(x == COLS - 1, from_down, from_up), carried), around)
    far = permute(half, half_way)

    def ids(distance, parity, ok):
        start = (frame + distance) * frame_blocks + slab * blocks + parity
        held = start + 2 * jnp.arange(blocks // 2, dtype=jnp.int32)
        return jnp.where(ok, held, -1)

    start = frame * frame_blocks + slab * blocks
    toward = 1 - 2 * core
    own_ids = start + jnp.arange(blocks, dtype=jnp.int32)
    halo_ids = jnp.stack(
        [
            jnp.where(slab > 0, start - 1, -1),
            jnp.where(slab < SPACE - 1, start + blocks, -1),
        ]
    )
    inner_edge = jnp.where(core == 0, 0, COLS - 1)
    inner_ok = jnp.where(core == 0, y > 0, y < ROWS - 1)
    lower = x < COLS // 2
    early_ids = jnp.concatenate(
        [
            own_ids,
            halo_ids,
            ids(toward, 0, True),
            ids(-toward, 0, x != inner_edge),
            ids(-toward, 0, (x == inner_edge) & inner_ok),
            ids(-8, 1, y > 0),
            ids(8, 1, y < ROWS - 1),
            ids(-2, 1, x > 0),
            ids(2, 1, x < COLS - 1),
            ids(jnp.where(lower, 4, -4), 0, True),
        ]
    )
    late_ids = jnp.concatenate(
        [
            ids(jnp.where(lower, -4, 4), 0, jnp.where(lower, y > 0, y < ROWS - 1)),
            ids(
                jnp.where(x == 0, -2, 2),
                1,
                ((x == 0) & (y > 0)) | ((x == COLS - 1) & (y < ROWS - 1)),
            ),
            ids(jnp.where(y < ROWS // 2, 16, -16), 0, True),
        ]
    )
    entry_live = jnp.arange(block_list.shape[1], dtype=jnp.int32)[None, :] < block_count[:, None]
    listed = jnp.where(entry_live, block_list, -2)

    def live(held):
        return jnp.any(listed[:, :, None] == held[None, None, :], axis=1).astype(jnp.int32)

    state = attend_early(
        live(early_ids),
        queries,
        key_rows,
        value_rows,
        below,
        above,
        [twin, near_chip, carried, from_down, from_up, from_left, from_right, two_chips],
    )
    return attend_late(live(late_ids), queries, state, [two_other, wrapped, far])


def solution(mesh):
    placed = (
        P(AXES, None),
        P(AXES, None),
        P(AXES, None),
        P(AXES, None),
        P(AXES),
    )
    return jax.shard_map(
        shards, mesh=mesh, in_specs=placed, out_specs=P(AXES, None), check_vma=False
    )
```

```python
import functools

import jax
import jax.numpy as jnp
from jax import lax
from jax.experimental import pallas as pl
from jax.experimental.pallas import tpu as pltpu
from jax.sharding import PartitionSpec as P

HEAD = 128
BLOCK = 128
ROWS = 4
COLS = 4
SPACE = 8
STEP_HEADS = 6
AT_ONCE = 2
PLAN = ('E1', 'U', 'D', 'D16', 'CS', 'E2:CS', 'ZP:CS', 'ZM:ZP', 'E3:ZM', 'RLa:E2,ZP', 'RLb:RLa,ZM', 'W:U,D,RLa', 'Y1:U,D,RLa')
PHASES = (('CS', 'E1', 'E2', 'U', 'D', 'RLa', 'ZP', 'ZM', 'D16'), ('RLb', 'E3'), ('Y1', 'W'))
NEG = -1e30
AXES = ("tm", "space")
barrier = lax.optimization_barrier


def device(y, x, core, z):
    return ((y % ROWS * COLS + x % COLS) * 2 + core) * SPACE + z


def permute(cells, move):
    pairs = []
    for y in range(ROWS):
        for x in range(COLS):
            for core in range(2):
                for z in range(SPACE):
                    place = move(y, x, core, z)
                    if place is not None:
                        pairs.append((device(y, x, core, z), device(*place)))
    return lax.ppermute(cells, AXES, pairs)


def up(y, x, core, z):
    return (y + 1, x, core, z) if y < ROWS - 1 else None


def down(y, x, core, z):
    return (y - 1, x, core, z) if y > 0 else None


def right(y, x, core, z):
    return (y, x + 1, core, z) if x < COLS - 1 else None


def left(y, x, core, z):
    return (y, x - 1, core, z) if x > 0 else None


def around(y, x, core, z):
    if x == COLS - 1 and y > 0:
        return (y, 0, core, z)
    if x == 0 and y < ROWS - 1:
        return (y, COLS - 1, core, z)
    return None


def ring_first(y, x, core, z):
    return (y, x + 1, 0, z) if core == 1 else (y, x - 1, 1, z)


def ring_second(y, x, core, z):
    return (y, x + 1, 1, z) if core == 0 else (y, x - 1, 0, z)


def carry(y, x, core, z):
    if x == 0 and core == 0 and y < ROWS - 1:
        return (y + 1, x, core, z)
    if x == COLS - 1 and core == 1 and y > 0:
        return (y - 1, x, core, z)
    return None


def other_row(y, x, core, z):
    if x < COLS // 2:
        return (y + 1, x, core, z) if y < ROWS - 1 else None
    return (y - 1, x, core, z) if y > 0 else None


def opposite(y, x, core, z):
    return (y + 2, x, core, z)


def split_out(y, x, core, z):
    return right(y, x, core, z) if core == 0 else left(y, x, core, z)


def split_in(y, x, core, z):
    return left(y, x, core, z) if core == 0 else right(y, x, core, z)


def other_core(y, x, core, z):
    return (y, x, 1 - core, z)


def next_slab(y, x, core, z):
    return (y, x, core, z + 1) if z < SPACE - 1 else None


def last_slab(y, x, core, z):
    return (y, x, core, z - 1) if z > 0 else None


def absorb(pick_ref, tile, first, held, q_ref, max_ref, sum_ref, acc_ref):
    scale = 1.4426950408889634 / HEAD**0.5
    picks = [pick_ref[tile, first + i] for i in range(AT_ONCE)]
    biases = [jnp.where(pick >= 0, 0.0, NEG) for pick in picks]
    picks = [jnp.maximum(pick, 0) for pick in picks]
    heads = range(STEP_HEADS)
    cols = [slice(head * HEAD, (head + 1) * HEAD) for head in heads]
    old = max_ref[tile, 0]
    scores, tops = [], []
    for head in heads:
        query = q_ref[tile, :, cols[head]]
        parts = [
            lax.dot_general(
                held[pick // 2, 0, pick % 2, :, cols[head]],
                query,
                (((1,), (1,)), ((), ())),
                preferred_element_type=jnp.float32,
            )
            * scale
            + bias
            for pick, bias in zip(picks, biases)
        ]
        both = functools.reduce(jnp.maximum, parts)
        tops.append(jnp.maximum(jnp.max(both, axis=0, keepdims=True), old[head : head + 1]))
        scores.append(jnp.concatenate(parts, axis=0))
    fades = [jnp.exp2(old[head : head + 1] - tops[head]) for head in heads]
    totals, accs = [], []
    for head in heads:
        weights = jnp.exp2(scores[head] - tops[head])
        totals.append(jnp.sum(weights, axis=0, keepdims=True))
        values = jnp.concatenate(
            [held[pick // 2, 1, pick % 2, :, cols[head]] for pick in picks], axis=0
        )
        mixed = lax.dot_general(
            values,
            weights.astype(jnp.bfloat16),
            (((0,), (0,)), ((), ())),
            preferred_element_type=jnp.float32,
        )
        accs.append(acc_ref[tile, cols[head], :] * fades[head] + mixed)
    sums = sum_ref[tile, 0] * jnp.concatenate(fades, axis=0) + jnp.concatenate(totals, axis=0)
    max_ref[tile, 0] = jnp.concatenate(tops, axis=0)
    sum_ref[tile, 0] = sums
    for head in heads:
        acc_ref[tile, cols[head], :] = accs[head]


def kernel(fresh, final, layout, pick_ref, q_ref, *rest):
    rest = list(rest)
    old = [] if fresh else [rest.pop(0) for _ in range(3)]
    arrays = [rest.pop(0) for _ in range(1 + max(part[0] for part in layout))]
    out_ref = rest.pop(0) if final else None
    max_ref, sum_ref, acc_ref, held, sems = rest
    step, steps = pl.program_id(0), pl.num_programs(0)
    wide = STEP_HEADS * HEAD

    def copies(at):
        slot = lax.rem(at, 2)
        cols = pl.ds(pl.multiple_of(at * wide, wide), wide)
        return [
            pltpu.make_async_copy(
                arrays[array].at[(*source, slice(None), cols)],
                held.at[(slot, *target)],
                sems.at[slot, index],
            )
            for index, (array, source, target) in enumerate(layout)
        ]

    @pl.when(step == 0)
    def _():
        for copy in copies(0):
            copy.start()

    @pl.when(step + 1 < steps)
    def _():
        for copy in copies(step + 1):
            copy.start()

    if fresh:
        max_ref[...] = jnp.full(max_ref.shape, NEG, jnp.float32)
        sum_ref[...] = jnp.zeros(sum_ref.shape, jnp.float32)
        acc_ref[...] = jnp.zeros(acc_ref.shape, jnp.float32)
    else:
        for new_ref, old_ref in zip((max_ref, sum_ref, acc_ref), old):
            new_ref[...] = old_ref[...]
    for copy in copies(step):
        copy.wait()
    tiles, entries = pick_ref.shape
    here = held.at[lax.rem(step, 2)]

    rounds = entries // AT_ONCE

    @pl.loop(0, tiles * rounds)
    def _(at):
        tile, first = at // rounds, at % rounds * AT_ONCE

        @pl.when(pick_ref[tile, first] >= 0)
        def _():
            absorb(pick_ref, tile, first, here, q_ref, max_ref, sum_ref, acc_ref)

    if final:
        for tile in range(tiles):
            for head in range(STEP_HEADS):
                cols = slice(head * HEAD, (head + 1) * HEAD)
                part = 1.0 / sum_ref[tile, 0, head : head + 1, :]
                done = (acc_ref[tile, cols, :] * part).astype(jnp.bfloat16)
                out_ref[tile, :, cols] = done.T


def attend(name, picks, queries, state, arrays, layout, final, flops):
    tiles, _, width = queries.shape
    wide = STEP_HEADS * HEAD
    steps = width // wide
    groups = 1 + max(target[0] for _, _, target in layout)
    rows = pl.BlockSpec((tiles, BLOCK, wide), lambda i: (0, 0, i))
    small = pl.BlockSpec((tiles, 1, STEP_HEADS, BLOCK), lambda i: (0, i, 0, 0))
    large = pl.BlockSpec((tiles, wide, BLOCK), lambda i: (0, i, 0))
    stats = jax.ShapeDtypeStruct((tiles, steps, STEP_HEADS, BLOCK), jnp.float32)
    total = jax.ShapeDtypeStruct((tiles, width, BLOCK), jnp.float32)
    scratch = [
        pltpu.VMEM((2, groups, 2, 2, BLOCK, wide), jnp.bfloat16),
        pltpu.SemaphoreType.DMA((2, len(layout))),
    ]
    if final:
        scratch = [
            pltpu.VMEM((tiles, 1, STEP_HEADS, BLOCK), jnp.float32),
            pltpu.VMEM((tiles, 1, STEP_HEADS, BLOCK), jnp.float32),
            pltpu.VMEM((tiles, wide, BLOCK), jnp.float32),
        ] + scratch
    return pl.pallas_call(
        functools.partial(kernel, not state, final, layout),
        grid=(steps,),
        in_specs=[pl.BlockSpec(memory_space=pltpu.SMEM), rows]
        + ([small, small, large] if state else [])
        + [pl.BlockSpec(memory_space=pl.ANY)] * len(arrays),
        out_specs=rows if final else [small, small, large],
        out_shape=jax.ShapeDtypeStruct(queries.shape, jnp.bfloat16)
        if final
        else (stats, stats, total),
        scratch_shapes=scratch,
        compiler_params=pltpu.CompilerParams(vmem_limit_bytes=56 * 1024 * 1024),
        cost_estimate=pl.CostEstimate(
            flops=flops, bytes_accessed=30_000_000, transcendentals=flops // 512
        ),
        name=name,
    )(picks, queries, *state, *arrays)


def shards(queries, key_rows, value_rows, block_list, block_count):
    rows, width = queries.shape
    blocks = rows // BLOCK
    frame_blocks = blocks * SPACE
    frame, slab = lax.axis_index("tm"), lax.axis_index("space")
    y, x, core = frame // (2 * COLS), frame // 2 % COLS, frame % 2

    tiled = queries.reshape(blocks, BLOCK, width)
    keys = key_rows.reshape(blocks, BLOCK, width)
    values = value_rows.reshape(blocks, BLOCK, width)
    even = jnp.stack([keys[0::2], values[0::2]])
    odd = jnp.stack([keys[1::2], values[1::2]])
    first = jnp.stack([keys[0], values[0]])
    last = jnp.stack([keys[blocks - 1], values[blocks - 1]])

    moves = {
        "U": (up, odd),
        "D": (down, odd),
        "RLa": (split_out, odd),
        "RLb": (split_in, odd),
        "W": (around, None),
        "E1": (ring_first, even),
        "E2": (ring_second, "E1"),
        "E3": (other_row, "E2"),
        "Y1": (carry, "E1"),
        "D16": (opposite, even),
        "CS": (other_core, even),
        "ZP": (next_slab, last),
        "ZM": (last_slab, first),
    }
    got = {}
    for step in PLAN:
        name, _, needs = step.partition(":")
        move, cells = moves[name]
        if isinstance(cells, str):
            cells = got[cells]
        elif cells is None:
            cells = jnp.where(x == COLS - 1, got["U"], got["D"])
        if needs:
            cells = barrier((cells, *[got[need] for need in needs.split(",")]))[0]
        got[name] = permute(cells, move)

    def ids(distance, parity, ok):
        start = (frame + distance) * frame_blocks + slab * blocks + parity
        held = start + 2 * jnp.arange(blocks // 2, dtype=jnp.int32)
        return jnp.where(ok, held, -1)

    start = frame * frame_blocks + slab * blocks
    toward = 1 - 2 * core
    own_ids = start + jnp.arange(blocks, dtype=jnp.int32)
    inner_edge = jnp.where(core == 0, 0, COLS - 1)
    inner_ok = jnp.where(core == 0, y > 0, y < ROWS - 1)
    lower = x < COLS // 2
    far_ids = ids(jnp.where(y < ROWS // 2, 16, -16), 0, True)
    carried_ids = ids(-toward, 0, (x == inner_edge) & inner_ok)
    group_ids = {
        "CS": ids(toward, 0, True),
        "E1": ids(-toward, 0, x != inner_edge),
        "Y1": carried_ids,
        "U": ids(-8, 1, y > 0),
        "D": ids(8, 1, y < ROWS - 1),
        "RLa": ids(-2 * toward, 1, jnp.where(core == 0, x > 0, x < COLS - 1)),
        "RLb": ids(2 * toward, 1, jnp.where(core == 0, x < COLS - 1, x > 0)),
        "ZP": jnp.stack([jnp.where(slab > 0, start - 1, -1), -1]),
        "ZM": jnp.stack([jnp.where(slab < SPACE - 1, start + blocks, -1), -1]),
        "W": ids(
            jnp.where(x == 0, -2, 2),
            1,
            ((x == 0) & (y > 0)) | ((x == COLS - 1) & (y < ROWS - 1)),
        ),
        "E2": ids(jnp.where(lower, 4, -4), 0, True),
        "E3": ids(jnp.where(lower, -4, 4), 0, jnp.where(lower, y > 0, y < ROWS - 1)),
        "D16": far_ids,
    }
    entry_live = jnp.arange(block_list.shape[1], dtype=jnp.int32)[None, :] < block_count[:, None]
    listed = jnp.where(entry_live, block_list, -2)

    def picks(held):
        match = listed[:, :, None] == held[None, None, :]
        found = jnp.any(match, axis=2)
        which = jnp.sum(jnp.where(match, jnp.arange(held.shape[0], dtype=jnp.int32), 0), axis=2)
        order = jnp.cumsum(found.astype(jnp.int32), axis=1) - 1
        places = jnp.arange(block_list.shape[1], dtype=jnp.int32)
        taken = (order[:, :, None] == places) & found[:, :, None]
        return jnp.sum(jnp.where(taken, which[:, :, None] + 1, 0), axis=1) - 1

    state = ()
    for index, names in enumerate(PHASES):
        arrays, held, layout = [], [], []
        if index == 0:
            arrays, held = [keys, values], [own_ids]
            layout = [
                (kv, (slice(2 * i, 2 * i + 2),), (i, kv))
                for i in range(blocks // 2)
                for kv in range(2)
            ]
        for name in names:
            group = sum(part.shape[0] for part in held) // 2
            layout += [
                (len(arrays), (kv,), (group, kv, 0))
                if name in ("ZP", "ZM")
                else (len(arrays), (kv, slice(None)), (group, kv))
                for kv in range(2)
            ]
            arrays.append(got[name])
            held.append(group_ids[name])
        state = attend(
            "phase" + str(index),
            picks(jnp.concatenate(held)),
            tiled,
            state,
            arrays,
            layout,
            index == len(PHASES) - 1,
            500_000_000 * len(held),
        )
    return state.reshape(rows, width)


def solution(mesh):
    placed = (
        P(AXES, None),
        P(AXES, None),
        P(AXES, None),
        P(AXES, None),
        P(AXES),
    )
    return jax.shard_map(
        shards, mesh=mesh, in_specs=placed, out_specs=P(AXES, None), check_vma=False
    )
```

```python
import functools

import jax
import jax.numpy as jnp
from jax import lax
from jax.experimental import pallas as pl
from jax.experimental.pallas import tpu as pltpu
from jax.sharding import PartitionSpec as P

HEAD = 128
BLOCK = 128
ROWS = 4
COLS = 4
SPACE = 8
STEP_HEADS = 6
AT_ONCE = 2
PLAN = ('E1', 'U', 'D', 'D16', 'CS', 'E2:CS', 'ZP:CS', 'ZM:ZP', 'E3:ZM', 'RLa:E2,ZP', 'RLb:RLa,ZM', 'W:U,D,RLa', 'Y1:U,D,RLa')
PHASES = (('CS', 'E1', 'E2', 'U', 'D', 'RLa', 'ZP', 'ZM', 'D16'), ('RLb', 'E3', 'W'), ('Y1',))
NEG = -1e30
AXES = ("tm", "space")
barrier = lax.optimization_barrier


def device(y, x, core, z):
    return ((y % ROWS * COLS + x % COLS) * 2 + core) * SPACE + z


def permute(cells, move):
    pairs = []
    for y in range(ROWS):
        for x in range(COLS):
            for core in range(2):
                for z in range(SPACE):
                    place = move(y, x, core, z)
                    if place is not None:
                        pairs.append((device(y, x, core, z), device(*place)))
    return lax.ppermute(cells, AXES, pairs)


def up(y, x, core, z):
    return (y + 1, x, core, z) if y < ROWS - 1 else None


def down(y, x, core, z):
    return (y - 1, x, core, z) if y > 0 else None


def right(y, x, core, z):
    return (y, x + 1, core, z) if x < COLS - 1 else None


def left(y, x, core, z):
    return (y, x - 1, core, z) if x > 0 else None


def around(y, x, core, z):
    if x == COLS - 1 and y > 0:
        return (y, 0, core, z)
    if x == 0 and y < ROWS - 1:
        return (y, COLS - 1, core, z)
    return None


def ring_first(y, x, core, z):
    return (y, x + 1, 0, z) if core == 1 else (y, x - 1, 1, z)


def ring_second(y, x, core, z):
    return (y, x + 1, 1, z) if core == 0 else (y, x - 1, 0, z)


def carry(y, x, core, z):
    if x == 0 and core == 0 and y < ROWS - 1:
        return (y + 1, x, core, z)
    if x == COLS - 1 and core == 1 and y > 0:
        return (y - 1, x, core, z)
    return None


def other_row(y, x, core, z):
    if x < COLS // 2:
        return (y + 1, x, core, z) if y < ROWS - 1 else None
    return (y - 1, x, core, z) if y > 0 else None


def opposite(y, x, core, z):
    return (y + 2, x, core, z)


def split_out(y, x, core, z):
    return right(y, x, core, z) if core == 0 else left(y, x, core, z)


def split_in(y, x, core, z):
    return left(y, x, core, z) if core == 0 else right(y, x, core, z)


def other_core(y, x, core, z):
    return (y, x, 1 - core, z)


def next_slab(y, x, core, z):
    return (y, x, core, z + 1) if z < SPACE - 1 else None


def last_slab(y, x, core, z):
    return (y, x, core, z - 1) if z > 0 else None


def absorb(pick_ref, tile, first, held, q_ref, max_ref, sum_ref, acc_ref):
    scale = 1.4426950408889634 / HEAD**0.5
    picks = [pick_ref[tile, first + i] for i in range(AT_ONCE)]
    biases = [jnp.where(pick >= 0, 0.0, NEG) for pick in picks]
    picks = [jnp.maximum(pick, 0) for pick in picks]
    heads = range(STEP_HEADS)
    cols = [slice(head * HEAD, (head + 1) * HEAD) for head in heads]
    old = max_ref[tile, 0]
    scores, tops = [], []
    for head in heads:
        query = q_ref[tile, :, cols[head]]
        parts = [
            lax.dot_general(
                held[pick // 2, 0, pick % 2, :, cols[head]],
                query,
                (((1,), (1,)), ((), ())),
                preferred_element_type=jnp.float32,
            )
            * scale
            + bias
            for pick, bias in zip(picks, biases)
        ]
        both = functools.reduce(jnp.maximum, parts)
        tops.append(jnp.maximum(jnp.max(both, axis=0, keepdims=True), old[head : head + 1]))
        scores.append(jnp.concatenate(parts, axis=0))
    fades = [jnp.exp2(old[head : head + 1] - tops[head]) for head in heads]
    totals, accs = [], []
    for head in heads:
        weights = jnp.exp2(scores[head] - tops[head])
        totals.append(jnp.sum(weights, axis=0, keepdims=True))
        values = jnp.concatenate(
            [held[pick // 2, 1, pick % 2, :, cols[head]] for pick in picks], axis=0
        )
        mixed = lax.dot_general(
            values,
            weights.astype(jnp.bfloat16),
            (((0,), (0,)), ((), ())),
            preferred_element_type=jnp.float32,
        )
        accs.append(acc_ref[tile, cols[head], :] * fades[head] + mixed)
    sums = sum_ref[tile, 0] * jnp.concatenate(fades, axis=0) + jnp.concatenate(totals, axis=0)
    max_ref[tile, 0] = jnp.concatenate(tops, axis=0)
    sum_ref[tile, 0] = sums
    for head in heads:
        acc_ref[tile, cols[head], :] = accs[head]


def kernel(fresh, final, layout, pick_ref, q_ref, *rest):
    rest = list(rest)
    old = [] if fresh else [rest.pop(0) for _ in range(3)]
    arrays = [rest.pop(0) for _ in range(1 + max(part[0] for part in layout))]
    out_ref = rest.pop(0) if final else None
    max_ref, sum_ref, acc_ref, held, sems = rest
    step, steps = pl.program_id(0), pl.num_programs(0)
    wide = STEP_HEADS * HEAD

    def copies(at):
        slot = lax.rem(at, 2)
        cols = pl.ds(pl.multiple_of(at * wide, wide), wide)
        return [
            pltpu.make_async_copy(
                arrays[array].at[(*source, slice(None), cols)],
                held.at[(slot, *target)],
                sems.at[slot, index],
            )
            for index, (array, source, target) in enumerate(layout)
        ]

    @pl.when(step == 0)
    def _():
        for copy in copies(0):
            copy.start()

    @pl.when(step + 1 < steps)
    def _():
        for copy in copies(step + 1):
            copy.start()

    if fresh:
        max_ref[...] = jnp.full(max_ref.shape, NEG, jnp.float32)
        sum_ref[...] = jnp.zeros(sum_ref.shape, jnp.float32)
        acc_ref[...] = jnp.zeros(acc_ref.shape, jnp.float32)
    else:
        for new_ref, old_ref in zip((max_ref, sum_ref, acc_ref), old):
            new_ref[...] = old_ref[...]
    for copy in copies(step):
        copy.wait()
    tiles, entries = pick_ref.shape
    here = held.at[lax.rem(step, 2)]

    rounds = entries // AT_ONCE

    @pl.loop(0, tiles * rounds)
    def _(at):
        tile, first = at // rounds, at % rounds * AT_ONCE

        @pl.when(pick_ref[tile, first] >= 0)
        def _():
            absorb(pick_ref, tile, first, here, q_ref, max_ref, sum_ref, acc_ref)

    if final:
        for tile in range(tiles):
            for head in range(STEP_HEADS):
                cols = slice(head * HEAD, (head + 1) * HEAD)
                part = 1.0 / sum_ref[tile, 0, head : head + 1, :]
                done = (acc_ref[tile, cols, :] * part).astype(jnp.bfloat16)
                out_ref[tile, :, cols] = done.T


def attend(name, picks, queries, state, arrays, layout, final, flops):
    tiles, _, width = queries.shape
    wide = STEP_HEADS * HEAD
    steps = width // wide
    groups = 1 + max(target[0] for _, _, target in layout)
    rows = pl.BlockSpec((tiles, BLOCK, wide), lambda i: (0, 0, i))
    small = pl.BlockSpec((tiles, 1, STEP_HEADS, BLOCK), lambda i: (0, i, 0, 0))
    large = pl.BlockSpec((tiles, wide, BLOCK), lambda i: (0, i, 0))
    stats = jax.ShapeDtypeStruct((tiles, steps, STEP_HEADS, BLOCK), jnp.float32)
    total = jax.ShapeDtypeStruct((tiles, width, BLOCK), jnp.float32)
    scratch = [
        pltpu.VMEM((2, groups, 2, 2, BLOCK, wide), jnp.bfloat16),
        pltpu.SemaphoreType.DMA((2, len(layout))),
    ]
    if final:
        scratch = [
            pltpu.VMEM((tiles, 1, STEP_HEADS, BLOCK), jnp.float32),
            pltpu.VMEM((tiles, 1, STEP_HEADS, BLOCK), jnp.float32),
            pltpu.VMEM((tiles, wide, BLOCK), jnp.float32),
        ] + scratch
    return pl.pallas_call(
        functools.partial(kernel, not state, final, layout),
        grid=(steps,),
        in_specs=[pl.BlockSpec(memory_space=pltpu.SMEM), rows]
        + ([small, small, large] if state else [])
        + [pl.BlockSpec(memory_space=pl.ANY)] * len(arrays),
        out_specs=rows if final else [small, small, large],
        out_shape=jax.ShapeDtypeStruct(queries.shape, jnp.bfloat16)
        if final
        else (stats, stats, total),
        scratch_shapes=scratch,
        compiler_params=pltpu.CompilerParams(vmem_limit_bytes=56 * 1024 * 1024),
        cost_estimate=pl.CostEstimate(
            flops=flops, bytes_accessed=30_000_000, transcendentals=flops // 512
        ),
        name=name,
    )(picks, queries, *state, *arrays)


def shards(queries, key_rows, value_rows, block_list, block_count):
    rows, width = queries.shape
    blocks = rows // BLOCK
    frame_blocks = blocks * SPACE
    frame, slab = lax.axis_index("tm"), lax.axis_index("space")
    y, x, core = frame // (2 * COLS), frame // 2 % COLS, frame % 2

    tiled = queries.reshape(blocks, BLOCK, width)
    keys = key_rows.reshape(blocks, BLOCK, width)
    values = value_rows.reshape(blocks, BLOCK, width)
    even = jnp.stack([keys[0::2], values[0::2]])
    odd = jnp.stack([keys[1::2], values[1::2]])
    first = jnp.stack([keys[0], values[0]])
    last = jnp.stack([keys[blocks - 1], values[blocks - 1]])

    moves = {
        "U": (up, odd),
        "D": (down, odd),
        "RLa": (split_out, odd),
        "RLb": (split_in, odd),
        "W": (around, None),
        "E1": (ring_first, even),
        "E2": (ring_second, "E1"),
        "E3": (other_row, "E2"),
        "Y1": (carry, "E1"),
        "D16": (opposite, even),
        "CS": (other_core, even),
        "ZP": (next_slab, last),
        "ZM": (last_slab, first),
    }
    got = {}
    for step in PLAN:
        name, _, needs = step.partition(":")
        move, cells = moves[name]
        if isinstance(cells, str):
            cells = got[cells]
        elif cells is None:
            cells = jnp.where(x == COLS - 1, got["U"], got["D"])
        if needs:
            cells = barrier((cells, *[got[need] for need in needs.split(",")]))[0]
        got[name] = permute(cells, move)

    def ids(distance, parity, ok):
        start = (frame + distance) * frame_blocks + slab * blocks + parity
        held = start + 2 * jnp.arange(blocks // 2, dtype=jnp.int32)
        return jnp.where(ok, held, -1)

    start = frame * frame_blocks + slab * blocks
    toward = 1 - 2 * core
    own_ids = start + jnp.arange(blocks, dtype=jnp.int32)
    inner_edge = jnp.where(core == 0, 0, COLS - 1)
    inner_ok = jnp.where(core == 0, y > 0, y < ROWS - 1)
    lower = x < COLS // 2
    far_ids = ids(jnp.where(y < ROWS // 2, 16, -16), 0, True)
    carried_ids = ids(-toward, 0, (x == inner_edge) & inner_ok)
    group_ids = {
        "CS": ids(toward, 0, True),
        "E1": ids(-toward, 0, x != inner_edge),
        "Y1": carried_ids,
        "U": ids(-8, 1, y > 0),
        "D": ids(8, 1, y < ROWS - 1),
        "RLa": ids(-2 * toward, 1, jnp.where(core == 0, x > 0, x < COLS - 1)),
        "RLb": ids(2 * toward, 1, jnp.where(core == 0, x < COLS - 1, x > 0)),
        "ZP": jnp.stack([jnp.where(slab > 0, start - 1, -1), -1]),
        "ZM": jnp.stack([jnp.where(slab < SPACE - 1, start + blocks, -1), -1]),
        "W": ids(
            jnp.where(x == 0, -2, 2),
            1,
            ((x == 0) & (y > 0)) | ((x == COLS - 1) & (y < ROWS - 1)),
        ),
        "E2": ids(jnp.where(lower, 4, -4), 0, True),
        "E3": ids(jnp.where(lower, -4, 4), 0, jnp.where(lower, y > 0, y < ROWS - 1)),
        "D16": far_ids,
    }
    entry_live = jnp.arange(block_list.shape[1], dtype=jnp.int32)[None, :] < block_count[:, None]
    listed = jnp.where(entry_live, block_list, -2)

    def picks(held):
        match = listed[:, :, None] == held[None, None, :]
        found = jnp.any(match, axis=2)
        which = jnp.sum(jnp.where(match, jnp.arange(held.shape[0], dtype=jnp.int32), 0), axis=2)
        order = jnp.cumsum(found.astype(jnp.int32), axis=1) - 1
        places = jnp.arange(block_list.shape[1], dtype=jnp.int32)
        taken = (order[:, :, None] == places) & found[:, :, None]
        return jnp.sum(jnp.where(taken, which[:, :, None] + 1, 0), axis=1) - 1

    state = ()
    for index, names in enumerate(PHASES):
        arrays, held, layout = [], [], []
        if index == 0:
            arrays, held = [keys, values], [own_ids]
            layout = [
                (kv, (slice(2 * i, 2 * i + 2),), (i, kv))
                for i in range(blocks // 2)
                for kv in range(2)
            ]
        for name in names:
            group = sum(part.shape[0] for part in held) // 2
            layout += [
                (len(arrays), (kv,), (group, kv, 0))
                if name in ("ZP", "ZM")
                else (len(arrays), (kv, slice(None)), (group, kv))
                for kv in range(2)
            ]
            arrays.append(got[name])
            held.append(group_ids[name])
        state = attend(
            "phase" + str(index),
            picks(jnp.concatenate(held)),
            tiled,
            state,
            arrays,
            layout,
            index == len(PHASES) - 1,
            500_000_000 * len(held),
        )
    return state.reshape(rows, width)


def solution(mesh):
    placed = (
        P(AXES, None),
        P(AXES, None),
        P(AXES, None),
        P(AXES, None),
        P(AXES),
    )
    return jax.shard_map(
        shards, mesh=mesh, in_specs=placed, out_specs=P(AXES, None), check_vma=False
    )
```
